32 devices in a mesh: expert: 8 (over y, x, core), dp: 4 (over z).
Axes of the slice: x: 2, y: 2, z: 4, core: 2. Of those that a mesh axis runs over, the one named last changes fastest.
Arguments:
- tokens: bfloat16 [4096, 2048], P(('expert', 'dp')), may hold values from -6 to 6
- expert_ids: int32 [4096, 8], P(('expert', 'dp')), may hold values from 0 to 63, all different within a row; in each aligned block of 128 rows (0 to 127, 128 to 255, ...) at most 20 rows name the same one
- gate_probs: float32 [4096, 8], P(('expert', 'dp')), may hold values from 0.02 to 0.4
- cotangent: bfloat16 [4096, 2048], P(('expert', 'dp')), may hold values from -6 to 6
- weight_in: bfloat16 [64, 2048, 768], P('expert'), may hold values from -0.125 to 0.125
- weight_down: bfloat16 [64, 384, 2048], P('expert'), may hold values from -0.3125 to 0.3125
- swap_flag: int32 [8], replicated, may hold values from 0 to 1, as said below
Outputs:
- layer_out: bfloat16 [4096, 2048], P(('expert', 'dp'))
- gate_grads: float32 [4096, 8], P(('expert', 'dp'))
- token_grads: bfloat16 [4096, 2048], P(('expert', 'dp'))
- grad_in: float32 [64, 2048, 768], P('expert', 'dp')
- grad_down: float32 [64, 384, 2048], P('expert', None, 'dp')
The draws below stay inside these ranges and needn't reach their ends.
Inputs may be any that keep to these rules, and one draw needn't show every extreme that they name: `expert_ids`: each row names 8 different experts. Among the 128 rows of one device no expert is named more than 20 times, and in some of these aligned blocks an expert is named exactly 20 times. swap_flag[i] = swap_flag[i XOR 2]. Where swap_flag[i] is 1, index i of the expert axis takes over the 8 experts of index i XOR 2; experts j * 8 to (j + 1) * 8 - 1 start on index j.
All inputs are finite; a program needn't handle non-finite values.
Results may differ from the reference program's by a relative error of at most 0.0085.
Values may be sent and summed in bfloat16 or wider, within the bound.
A program may use at most 192 MiB of HBM per device.

```python
import math
import jax
import jax.numpy as jnp
import numpy as np
from jax import lax

D = 2048
FF = 384
EXPERTS = 64
TOP = 8
TOK_DEV = 128
CAP = 20
EXP_DEV = 8
TOKENS = 4096
N_EXPERT = 8
N_DP = 4


def draw_swap_flag(key, part):
    raw_flags = jax.random.randint(key, (N_EXPERT,), 0, 2, dtype=jnp.int32)
    raw_flags = raw_flags.at[0].set(1).at[1].set(0)
    positions = jnp.arange(N_EXPERT, dtype=jnp.int32)
    partner = jnp.bitwise_xor(positions, 2)
    return raw_flags[jnp.minimum(positions, partner)]


def shard_levels(stream_key, dims, shards, least, top_value):
    def one(position, blocks):
        heights = jax.random.uniform(jax.random.fold_in(jax.random.fold_in(stream_key, 6), position), (blocks,), jnp.float32, least / len(shards), top_value / len(shards))
        return jnp.repeat(jnp.exp(heights), dims[position] // blocks).reshape((-1,) + (1,) * (len(dims) - position - 1))

    level = one(*shards[0])
    for cut in shards[1:]:
        level = level * one(*cut)
    return level


def shared_out(rng, own, number, rows, count, top, limit, skew):
    sequence = jax.random.permutation(rng, count)
    heavy_load, usual = load_shares(count, rows * top, limit, skew, True), load_shares(count, rows * top, limit, skew, False)
    places = jnp.arange(count)

    def named(lengths, offset_by):
        used = int((lengths > 0).sum())
        fixed = max(1, used // 4)
        shifted = fixed + (places - fixed + offset_by * (used - fixed)) % max(1, count - fixed)
        return jnp.zeros((count,), jnp.int32).at[sequence[jnp.where(places < fixed, places, shifted)]].set(jnp.asarray(lengths, jnp.int32))

    lengths = jnp.where(number % 4 == 0, named(heavy_load, number // 4), named(usual, number - number // 4 - 1))
    mixed = jax.random.permutation(jax.random.fold_in(own, 3), count)
    source_of, receiver = mixed[0:count // 2 * 2:2], mixed[1:count // 2 * 2:2]
    room = jnp.minimum(lengths[source_of] - 1, limit - lengths[receiver]) // 2
    room = jnp.where((source_of == sequence[0]) | (receiver == sequence[0]) | (lengths[receiver] == 0), 0, jnp.maximum(room, 0))
    shifted = jax.random.randint(jax.random.fold_in(own, 4), (count // 2,), 0, 1 << 20) % (room + 1)
    lengths = lengths.at[source_of].add(-shifted).at[receiver].add(shifted)
    labels = jnp.searchsorted(jnp.cumsum(lengths), jnp.arange(rows * top), side="right").astype(jnp.int32)
    listing = labels.reshape(top, rows).T
    listing = listing[jax.random.permutation(jax.random.fold_in(own, 1), rows)]
    offset_by = jax.random.randint(jax.random.fold_in(own, 2), (rows, 1), 0, top)
    return jnp.take_along_axis(listing, (jnp.arange(top)[None, :] + offset_by) % top, axis=1)


def load_shares(count, total, bound, slope, full):
    weights = [(1 << 20) // math.isqrt(rank ** slope) + 1 for rank in range(1, count + 1)]
    largest = bound if full else min(bound, max(-(-total // count), total * weights[0] // sum(weights)))
    least = 1 if total - largest >= count - 1 else 0
    holding, rest = [largest] + [least] * (count - 1), total - largest - least * (count - 1)
    while rest > 0:
        free = [i for i in range(1, count) if holding[i] < largest] or [i for i in range(1, count) if holding[i] < bound]
        pool, budget = sum([weights[i] for i in free]), rest
        for i in free:
            extra = min(bound - holding[i], max(1, budget * weights[i] // pool), rest)
            holding[i] = holding[i] + extra
            rest = rest - extra
    return np.array(holding)


def bell_draw(own_key, shape, scale, bound, pieces=(), kind=jnp.bfloat16):
    array = jax.random.normal(own_key, shape, jnp.float32) * scale
    if len(pieces) > 0:
        array = shard_levels(own_key, shape, pieces, -0.22, 0.18) * array
    return jnp.clip(array, min=-bound, max=bound).astype(kind)


def setup_inputs(seed: int = 0) -> dict:
    seeds = jax.random.split(jax.random.key(seed), 8)
    tokens = bell_draw(seeds[0], (TOKENS, D), 1.0, 6.0, ((0, 32),))
    expert_ids_keys = jax.random.split(jax.random.fold_in(seeds[1], 1), TOKENS // TOK_DEV)
    expert_ids_turns = jax.random.permutation(jax.random.fold_in(seeds[1], 3), TOKENS // TOK_DEV)
    expert_ids = jax.vmap(lambda own, number: shared_out(jax.random.fold_in(seeds[1], 2), own, number, TOK_DEV, EXPERTS, TOP, CAP, 2))(expert_ids_keys, expert_ids_turns).reshape((TOKENS, TOP))
    gate_probs = jnp.clip(jnp.exp(math.log(0.4) - 2.9957323 * jax.random.uniform(seeds[2], (TOKENS, TOP), jnp.float32) ** shard_levels(seeds[2], (TOKENS, TOP), ((0, 32),), -0.2, 0.2)), 0.02, 0.4)
    cotangent = bell_draw(seeds[3], (TOKENS, D), 1.0, 6.0, ((0, 32),))
    weight_in = bell_draw(seeds[4], (EXPERTS, D, 2 * FF), D ** -0.5, 0.125, ((0, 8),))
    weight_down = bell_draw(seeds[5], (EXPERTS, FF, D), FF ** -0.5, 0.3125, ((0, 8),))
    swap_flag = draw_swap_flag(jax.random.fold_in(seeds[7], 71), 0)
    return dict(tokens=tokens, expert_ids=expert_ids, gate_probs=gate_probs, cotangent=cotangent, weight_in=weight_in, weight_down=weight_down, swap_flag=swap_flag)


def expert_pass(rows_x, rows_grad, first_weight, second_weight):
    projected = jnp.dot(rows_x, first_weight, preferred_element_type=jnp.float32)
    width = second_weight.shape[0]
    pre_gate = projected[:, :width]
    up_part = projected[:, width:]
    sigmoid_gate = jax.nn.sigmoid(pre_gate)
    activated = pre_gate * sigmoid_gate
    hidden = (activated * up_part).astype(jnp.bfloat16)
    expert_out = jnp.dot(hidden, second_weight, preferred_element_type=jnp.float32).astype(jnp.bfloat16)
    hidden_grad = jnp.dot(rows_grad, second_weight.T, preferred_element_type=jnp.float32)
    gate_grad = hidden_grad * up_part * sigmoid_gate * (1.0 + pre_gate * (1.0 - sigmoid_gate))
    proj_grad = jnp.concatenate([gate_grad, hidden_grad * activated], axis=-1).astype(jnp.bfloat16)
    row_grad = jnp.dot(proj_grad, first_weight.T, preferred_element_type=jnp.float32).astype(jnp.bfloat16)
    return hidden, expert_out, proj_grad, row_grad


def reference(tokens, expert_ids, gate_probs, cotangent, weight_in, weight_down, swap_flag):
    assigned = TOKENS * TOP
    blocks = N_EXPERT * N_DP
    flat_ids = expert_ids.reshape(-1).astype(jnp.int32)
    onehot = (flat_ids[:, None] == jnp.arange(EXPERTS, dtype=jnp.int32)[None, :]).astype(jnp.int32)
    onehot = onehot.reshape(blocks, TOK_DEV * TOP, EXPERTS)
    earlier = jnp.cumsum(onehot, axis=1) - onehot
    slot_rank = jnp.sum(earlier * onehot, axis=2).reshape(-1).astype(jnp.int32)
    block_of = (jnp.arange(assigned, dtype=jnp.int32) // (TOK_DEV * TOP)).astype(jnp.int32)
    slot_index = (flat_ids * (blocks * CAP) + block_of * CAP + slot_rank).astype(jnp.int32)
    table = jnp.full((EXPERTS * blocks * CAP,), assigned, jnp.int32)
    table = table.at[slot_index].set(jnp.arange(assigned, dtype=jnp.int32))
    table = table.reshape(EXPERTS, blocks * CAP)
    tokens_pad = jnp.concatenate([tokens, jnp.zeros((1, D), tokens.dtype)], axis=0)
    cot_pad = jnp.concatenate([cotangent, jnp.zeros((1, D), cotangent.dtype)], axis=0)
    probs_pad = jnp.concatenate([gate_probs.reshape(-1), jnp.zeros((1,), gate_probs.dtype)])

    def per_expert(carry, inputs):
        layer_acc, grad_acc, gate_acc = carry
        rows, first_weight, second_weight = inputs
        token_of = (rows // TOP).astype(jnp.int32)
        rows_x = tokens_pad[token_of]
        rows_prob = probs_pad[rows]
        rows_cot = cot_pad[token_of].astype(jnp.float32)
        rows_grad = (rows_prob[:, None] * rows_cot).astype(jnp.bfloat16)
        hidden, expert_out, proj_grad, row_grad = expert_pass(rows_x, rows_grad, first_weight, second_weight)
        out_wide = expert_out.astype(jnp.float32)
        layer_acc = layer_acc.at[token_of].add(rows_prob[:, None] * out_wide)
        grad_acc = grad_acc.at[token_of].add(row_grad.astype(jnp.float32))
        gate_acc = gate_acc.at[rows].set(jnp.sum(rows_cot * out_wide, axis=1))
        x_four = rows_x.reshape(N_EXPERT, N_DP, CAP, D).astype(jnp.float32)
        pg_four = proj_grad.reshape(N_EXPERT, N_DP, CAP, 2 * FF).astype(jnp.float32)
        hid_four = hidden.reshape(N_EXPERT, N_DP, CAP, FF).astype(jnp.float32)
        og_four = rows_grad.reshape(N_EXPERT, N_DP, CAP, D).astype(jnp.float32)
        replica_in = jnp.einsum('idcx,idcf->dxf', x_four, pg_four, precision=lax.Precision.HIGHEST)
        replica_down = jnp.einsum('idcf,idcx->dfx', hid_four, og_four, precision=lax.Precision.HIGHEST)
        replica_in = lax.optimization_barrier(replica_in.astype(jnp.bfloat16))
        replica_down = lax.optimization_barrier(replica_down.astype(jnp.bfloat16))
        summed_in = jnp.sum(replica_in.astype(jnp.float32), axis=0)
        summed_down = jnp.sum(replica_down.astype(jnp.float32), axis=0)
        return (layer_acc, grad_acc, gate_acc), (summed_in, summed_down)

    start = (jnp.zeros((TOKENS + 1, D), jnp.float32), jnp.zeros((TOKENS + 1, D), jnp.float32), jnp.zeros((assigned + 1,), jnp.float32))
    finals, stacked = lax.scan(per_expert, start, (table, weight_in, weight_down))
    layer_acc, grad_acc, gate_acc = finals
    grads_in, grads_down = stacked
    layer_out = layer_acc[:TOKENS].astype(jnp.bfloat16)
    token_grads = grad_acc[:TOKENS].astype(jnp.bfloat16)
    gate_grads = gate_acc[:assigned].reshape(TOKENS, TOP)
    slot_ids = jnp.arange(EXPERTS, dtype=jnp.int32)
    device_of = (slot_ids // EXP_DEV).astype(jnp.int32)
    moved = swap_flag.astype(jnp.int32)[device_of]
    held_expert = (jnp.bitwise_xor(device_of, 2 * moved) * EXP_DEV + slot_ids % EXP_DEV).astype(jnp.int32)
    return layer_out, gate_grads, token_grads, grads_in[held_expert], grads_down[held_expert]
```

```python
import jax
import jax.numpy as jnp
from jax import lax
from jax.sharding import PartitionSpec as P

FF = 384
EXPERTS = 64
TOP = 8
CAP = 20


def swapped(block, axis, apart):
    count = lax.axis_size(axis)
    route = []
    for low in range(count):
        high = low | 1 << apart
        if high != low and high < count:
            route += [(low, high), (high, low)]
    return lax.ppermute(block, axis, route)


def body(tokens, expert_ids, gate_probs, cotangent, weight_in, weight_down, swap_flag):
    row_count = tokens.shape[0]
    model_width = tokens.shape[1]
    per_device = weight_in.shape[0]
    groups = lax.axis_size("expert")
    replicas = lax.axis_size("dp")
    part_width = model_width // replicas
    device_ids = jnp.arange(groups, dtype=jnp.int32)
    my_index = lax.axis_index("expert")
    my_flag = jnp.sum(jnp.where(device_ids == my_index, swap_flag, 0))
    expert_range = jnp.arange(EXPERTS, dtype=jnp.int32)
    home_device = expert_range // per_device
    moved_flag = jnp.sum(
        jnp.where(home_device[:, None] == device_ids[None, :], swap_flag[None, :], 0), axis=1
    )
    target_device = jnp.bitwise_xor(home_device, 2 * moved_flag)
    dest_place = target_device * per_device + expert_range % per_device

    onehot = expert_ids[:, :, None] == expert_range[None, None, :]
    named = jnp.sum(onehot.astype(jnp.bfloat16), axis=1)
    token_range = jnp.arange(row_count, dtype=jnp.int32)
    earlier = (token_range[:, None] > token_range[None, :]).astype(jnp.bfloat16)
    rank_table = jnp.dot(earlier, named, preferred_element_type=jnp.float32).astype(jnp.int32)
    slot_rank = jnp.sum(jnp.where(onehot, rank_table[:, None, :], 0), axis=2)
    place_of = jnp.sum(jnp.where(onehot, dest_place[None, None, :], 0), axis=2)
    slot_index = (expert_ids * CAP + slot_rank).reshape(-1)

    my_replica = lax.axis_index("dp")
    part_index = (place_of * replicas + my_replica) * CAP + slot_rank
    route = jnp.concatenate([part_index.astype(jnp.float32), gate_probs], axis=1)
    route = lax.all_gather(route, "dp", axis=0, tiled=True)
    part_index = route[:, :TOP].astype(jnp.int32).reshape(-1)
    part_probs = route[:, TOP:]
    both = jnp.stack([tokens, cotangent])
    both = lax.all_to_all(both, "dp", split_axis=2, concat_axis=1, tiled=True)

    token_copies = jnp.repeat(tokens, TOP, axis=0)
    grad_rows = (gate_probs[:, :, None] * cotangent[:, None, :].astype(jnp.float32)).astype(
        jnp.bfloat16
    )
    grad_rows = grad_rows.reshape(row_count * TOP, model_width)
    empty_rows = jnp.zeros((EXPERTS * CAP, model_width), jnp.bfloat16)
    send_x = (
        empty_rows.at[slot_index].set(token_copies).reshape(groups, per_device, CAP, model_width)
    )
    send_grad = (
        empty_rows.at[slot_index].set(grad_rows).reshape(groups, per_device, CAP, model_width)
    )
    recv_x = lax.all_to_all(send_x, "expert", split_axis=0, concat_axis=0, tiled=True)
    recv_grad = lax.all_to_all(send_grad, "expert", split_axis=0, concat_axis=0, tiled=True)

    part_x = jnp.repeat(both[0], TOP, axis=0)
    part_grad = (part_probs[:, :, None] * both[1][:, None, :].astype(jnp.float32)).astype(
        jnp.bfloat16
    )
    part_grad = part_grad.reshape(replicas * row_count * TOP, part_width)
    part_rows = jnp.concatenate([part_x, part_grad], axis=1)
    send_part = (
        jnp.zeros((EXPERTS * replicas * CAP, 2 * part_width), jnp.bfloat16)
        .at[part_index]
        .set(part_rows)
        .reshape(groups, per_device, replicas, CAP, 2 * part_width)
    )
    recv_part = lax.all_to_all(send_part, "expert", split_axis=0, concat_axis=0, tiled=True)

    projected = jnp.einsum("nscd,sdf->nscf", recv_x, weight_in, preferred_element_type=jnp.float32)
    pre_gate = projected[..., :FF]
    up_part = projected[..., FF:]
    sigmoid_gate = jax.nn.sigmoid(pre_gate)
    activated = pre_gate * sigmoid_gate
    hidden = (activated * up_part).astype(jnp.bfloat16)
    hidden_moved = jnp.where(my_flag == 1, swapped(hidden, "expert", 1), hidden)
    hidden_all = lax.all_gather(hidden_moved, "dp", axis=0)
    expert_out = jnp.einsum(
        "nscf,sfd->nscd", hidden, weight_down, preferred_element_type=jnp.float32
    ).astype(jnp.bfloat16)
    hidden_grad = jnp.einsum(
        "nscd,sfd->nscf", recv_grad, weight_down, preferred_element_type=jnp.float32
    )
    gate_grad = hidden_grad * up_part * sigmoid_gate * (1.0 + pre_gate * (1.0 - sigmoid_gate))
    proj_grad = jnp.concatenate([gate_grad, hidden_grad * activated], axis=-1).astype(jnp.bfloat16)
    proj_moved = jnp.where(my_flag == 1, swapped(proj_grad, "expert", 1), proj_grad)
    proj_all = lax.all_gather(proj_moved, "dp", axis=0)
    row_grad = jnp.einsum(
        "nscf,sdf->nscd", proj_grad, weight_in, preferred_element_type=jnp.float32
    ).astype(jnp.bfloat16)
    home_out = lax.all_to_all(expert_out, "expert", split_axis=0, concat_axis=0, tiled=True)
    home_grad = lax.all_to_all(row_grad, "expert", split_axis=0, concat_axis=0, tiled=True)

    grad_first = jnp.einsum(
        "nsrcd,rnscf->sdf",
        recv_part[..., :part_width],
        proj_all,
        preferred_element_type=jnp.float32,
    )
    grad_second = jnp.einsum(
        "rnscf,nsrcd->sfd",
        hidden_all,
        recv_part[..., part_width:],
        preferred_element_type=jnp.float32,
    )

    out_rows = home_out.reshape(EXPERTS * CAP, model_width)[slot_index]
    out_rows = out_rows.astype(jnp.float32).reshape(row_count, TOP, model_width)
    layer_out = jnp.sum(gate_probs[:, :, None] * out_rows, axis=1).astype(jnp.bfloat16)
    gate_grads = jnp.sum(cotangent[:, None, :].astype(jnp.float32) * out_rows, axis=2)
    back_rows = home_grad.reshape(EXPERTS * CAP, model_width)[slot_index]
    back_rows = back_rows.astype(jnp.float32).reshape(row_count, TOP, model_width)
    token_grads = jnp.sum(back_rows, axis=1).astype(jnp.bfloat16)
    return (layer_out, gate_grads, token_grads, grad_first, grad_second)


def solution(mesh):
    in_specs = (
        P(("expert", "dp"), None),
        P(("expert", "dp"), None),
        P(("expert", "dp"), None),
        P(("expert", "dp"), None),
        P("expert", None, None),
        P("expert", None, None),
        P(),
    )
    out_specs = (
        P(("expert", "dp"), None),
        P(("expert", "dp"), None),
        P(("expert", "dp"), None),
        P("expert", "dp", None),
        P("expert", None, "dp"),
    )
    return jax.shard_map(body, mesh=mesh, in_specs=in_specs, out_specs=out_specs, check_vma=False)
```

```python
import jax
import jax.numpy as jnp
from jax import lax
from jax.sharding import PartitionSpec as P

FF = 384
EXPERTS = 64
TOP = 8
CAP = 20


def swapped(block, axis, apart):
    count = lax.axis_size(axis)
    route = []
    for low in range(count):
        high = low | 1 << apart
        if high != low and high < count:
            route += [(low, high), (high, low)]
    return lax.ppermute(block, axis, route)


def body(tokens, expert_ids, gate_probs, cotangent, weight_in, weight_down, swap_flag):
    row_count = tokens.shape[0]
    model_width = tokens.shape[1]
    per_device = weight_in.shape[0]
    groups = lax.axis_size("expert")
    replicas = lax.axis_size("dp")
    part_width = model_width // replicas
    device_ids = jnp.arange(groups, dtype=jnp.int32)
    my_index = lax.axis_index("expert")
    my_flag = jnp.sum(jnp.where(device_ids == my_index, swap_flag, 0))
    expert_range = jnp.arange(EXPERTS, dtype=jnp.int32)
    home_device = expert_range // per_device
    moved_flag = jnp.sum(
        jnp.where(home_device[:, None] == device_ids[None, :], swap_flag[None, :], 0), axis=1
    )
    target_device = jnp.bitwise_xor(home_device, 2 * moved_flag)
    dest_place = target_device * per_device + expert_range % per_device

    onehot = expert_ids[:, :, None] == expert_range[None, None, :]
    named = jnp.sum(onehot.astype(jnp.bfloat16), axis=1)
    token_range = jnp.arange(row_count, dtype=jnp.int32)
    earlier = (token_range[:, None] > token_range[None, :]).astype(jnp.bfloat16)
    rank_table = jnp.dot(earlier, named, preferred_element_type=jnp.float32).astype(jnp.int32)
    slot_rank = jnp.sum(jnp.where(onehot, rank_table[:, None, :], 0), axis=2)
    place_of = jnp.sum(jnp.where(onehot, dest_place[None, None, :], 0), axis=2)
    slot_index = (expert_ids // per_device * CAP + slot_rank) * per_device
    slot_index = (slot_index + expert_ids % per_device).reshape(-1)

    my_replica = lax.axis_index("dp")
    part_index = (place_of // per_device * replicas + my_replica) * CAP + slot_rank
    part_index = part_index * per_device + place_of % per_device
    route = jnp.concatenate([part_index.astype(jnp.float32), gate_probs], axis=1)
    route = jnp.broadcast_to(route[None], (replicas,) + route.shape)
    route = lax.all_to_all(route, "dp", split_axis=0, concat_axis=0, tiled=True)
    route = route.reshape(replicas * row_count, 2 * TOP)
    both = jnp.stack([tokens, cotangent])
    both = lax.all_to_all(both, "dp", split_axis=2, concat_axis=1, tiled=True)

    token_copies = jnp.repeat(tokens, TOP, axis=0)
    grad_rows = (gate_probs[:, :, None] * cotangent[:, None, :].astype(jnp.float32)).astype(
        jnp.bfloat16
    )
    grad_rows = grad_rows.reshape(row_count * TOP, model_width)
    empty_rows = jnp.zeros((EXPERTS * CAP, model_width), jnp.bfloat16)
    send_x = (
        empty_rows.at[slot_index].set(token_copies).reshape(groups, CAP, per_device, model_width)
    )
    send_grad = (
        empty_rows.at[slot_index].set(grad_rows).reshape(groups, CAP, per_device, model_width)
    )
    send_x, both, route = lax.optimization_barrier((send_x, both, route))
    recv_x = lax.all_to_all(send_x, "expert", split_axis=0, concat_axis=0, tiled=True)
    recv_grad = lax.all_to_all(send_grad, "expert", split_axis=0, concat_axis=0, tiled=True)

    part_index = route[:, :TOP].astype(jnp.int32).reshape(-1)
    part_probs = route[:, TOP:]
    part_x = jnp.repeat(both[0], TOP, axis=0)
    part_grad = (part_probs[:, :, None] * both[1][:, None, :].astype(jnp.float32)).astype(
        jnp.bfloat16
    )
    part_grad = part_grad.reshape(replicas * row_count * TOP, part_width)
    part_rows = jnp.concatenate([part_x, part_grad], axis=1)
    send_part = (
        jnp.zeros((EXPERTS * replicas * CAP, 2 * part_width), jnp.bfloat16)
        .at[part_index]
        .set(part_rows)
        .reshape(groups, replicas, CAP, per_device, 2 * part_width)
    )

    projected = jnp.einsum("ncsd,sdf->ncsf", recv_x, weight_in, preferred_element_type=jnp.float32)
    pre_gate = projected[..., :FF]
    up_part = projected[..., FF:]
    sigmoid_gate = jax.nn.sigmoid(pre_gate)
    activated = pre_gate * sigmoid_gate
    hidden = (activated * up_part).astype(jnp.bfloat16)
    hidden_moved = jnp.where(my_flag == 1, swapped(hidden, "expert", 1), hidden)
    hidden_moved, send_part, recv_grad = lax.optimization_barrier(
        (hidden_moved, send_part, recv_grad)
    )
    hidden_all = lax.all_gather(hidden_moved, "dp", axis=0)
    expert_out = jnp.einsum(
        "ncsf,sfd->ncsd", hidden, weight_down, preferred_element_type=jnp.float32
    ).astype(jnp.bfloat16)
    hidden_grad = jnp.einsum(
        "ncsd,sfd->ncsf", recv_grad, weight_down, preferred_element_type=jnp.float32
    )
    gate_grad = hidden_grad * up_part * sigmoid_gate * (1.0 + pre_gate * (1.0 - sigmoid_gate))
    proj_grad = jnp.concatenate([gate_grad, hidden_grad * activated], axis=-1).astype(jnp.bfloat16)
    proj_moved = jnp.where(my_flag == 1, swapped(proj_grad, "expert", 1), proj_grad)
    row_grad = jnp.einsum(
        "ncsf,sdf->ncsd", proj_grad, weight_in, preferred_element_type=jnp.float32
    ).astype(jnp.bfloat16)
    home_out = lax.all_to_all(expert_out, "expert", split_axis=0, concat_axis=0, tiled=True)
    proj_moved, hidden_all, row_grad, send_part = lax.optimization_barrier(
        (proj_moved, hidden_all, row_grad, send_part)
    )
    proj_all = lax.all_gather(proj_moved, "dp", axis=0)
    recv_part = lax.all_to_all(send_part, "expert", split_axis=0, concat_axis=0, tiled=True)
    home_grad = lax.all_to_all(row_grad, "expert", split_axis=0, concat_axis=0, tiled=True)
    proj_all, home_grad = lax.optimization_barrier((proj_all, home_grad))

    grad_first = jnp.einsum(
        "nrcsd,rncsf->sdf",
        recv_part[..., :part_width],
        proj_all,
        preferred_element_type=jnp.float32,
    )
    grad_second = jnp.einsum(
        "rncsf,nrcsd->sfd",
        hidden_all,
        recv_part[..., part_width:],
        preferred_element_type=jnp.float32,
    )

    out_rows = home_out.reshape(EXPERTS * CAP, model_width)[slot_index]
    out_rows = out_rows.astype(jnp.float32).reshape(row_count, TOP, model_width)
    layer_out = jnp.sum(gate_probs[:, :, None] * out_rows, axis=1).astype(jnp.bfloat16)
    gate_grads = jnp.sum(cotangent[:, None, :].astype(jnp.float32) * out_rows, axis=2)
    back_rows = home_grad.reshape(EXPERTS * CAP, model_width)[slot_index]
    back_rows = back_rows.astype(jnp.float32).reshape(row_count, TOP, model_width)
    token_grads = jnp.sum(back_rows, axis=1).astype(jnp.bfloat16)
    return (layer_out, gate_grads, token_grads, grad_first, grad_second)


def solution(mesh):
    in_specs = (
        P(("expert", "dp"), None),
        P(("expert", "dp"), None),
        P(("expert", "dp"), None),
        P(("expert", "dp"), None),
        P("expert", None, None),
        P("expert", None, None),
        P(),
    )
    out_specs = (
        P(("expert", "dp"), None),
        P(("expert", "dp"), None),
        P(("expert", "dp"), None),
        P("expert", "dp", None),
        P("expert", None, "dp"),
    )
    return jax.shard_map(body, mesh=mesh, in_specs=in_specs, out_specs=out_specs, check_vma=False)
```
